512 devices in a mesh: group: 16 (over x_hi, z), member: 32 (over y, x_lo, core).
Axes of the slice: x: 4 (x_hi: 2, x_lo: 2; x = x_hi * 2 + x_lo), y: 8, z: 8, core: 2. Of those that a mesh axis runs over, the one named last changes fastest.
Arguments:
- points: bfloat16 [9, 524288], P(None, ('group', 'member')), may hold values from -4 to 4
- probes: bfloat16 [8, 524288], P(None, ('group', 'member')), may hold values from -40 to 40
- col_blocks: int32 [16, 32, 20], P('group', 'member'), may hold values from 0 to 31, as said below
Outputs:
- product_out: float32 [8, 524288], P(None, ('group', 'member'))
- curvature_out: float32 [8], replicated
The draws below stay inside these ranges and needn't reach their ends.
Inputs may be any that keep to these rules, and one draw needn't show every extreme that they name: `col_blocks`: the 20 numbers of each row of the last dimension are different.
All inputs are finite; a program needn't handle non-finite values.
Results may differ from the reference program's by a relative error of at most 0.0027.
Values may be sent and summed in bfloat16 or wider, within the bound.
A program may use at most 64 MiB of HBM per device.

```python
import jax
import jax.numpy as jnp
from jax import lax

DIMS = 9
RHS = 8
P_DEV = 1024
GROUPS = 16
MEMBERS = 32
TPD = 20
NPTS = 524288


def draw_probes(key, part):
    key = jax.random.fold_in(key, 1)
    first_key, second_key = jax.random.split(key)
    row_scales = 10.0 ** (jnp.arange(RHS, dtype=jnp.float32) / (RHS - 1))
    position = jnp.arange(NPTS, dtype=jnp.float32) / (NPTS - 1)
    roughness = 10.0 ** jax.random.uniform(second_key, (NPTS,), dtype=jnp.float32)
    values = jax.random.truncated_normal(first_key, -4.0, 4.0, (RHS, NPTS), dtype=jnp.float32)
    rising = 3.0 ** position
    return (0.015 * values * row_scales[:, None] * (roughness * rising)[None, :]).astype(jnp.bfloat16)


def draw_col_blocks(key, part):
    key = jax.random.fold_in(key, 2)
    scores = jax.random.randint(key, (GROUPS, MEMBERS, MEMBERS), 0, 1 << 20) * MEMBERS + jnp.arange(MEMBERS, dtype=jnp.int32)
    ordering = jnp.argsort(scores, axis=-1, stable=True).astype(jnp.int32)
    return ordering[:, :, :TPD]


def block_scale(stream_key, dims, shards, smallest, largest):
    def one(axis_at, blocks):
        steps = jax.random.uniform(jax.random.fold_in(jax.random.fold_in(stream_key, 6), axis_at), (blocks,), jnp.float32, smallest / len(shards), largest / len(shards))
        return jnp.repeat(jnp.exp(steps), dims[axis_at] // blocks).reshape((-1,) + (1,) * (len(dims) - axis_at - 1))

    factor_of = one(*shards[0])
    for cut in shards[1:]:
        factor_of = factor_of * one(*cut)
    return factor_of


def bell_draw(key, shape, width, reach, cuts=(), kind=jnp.bfloat16):
    entries = jax.random.normal(key, shape, jnp.float32) * width
    if len(cuts) > 0:
        entries = block_scale(key, shape, cuts, -0.22, 0.18) * entries
    return jnp.clip(entries, min=-reach, max=reach).astype(kind)


def setup_inputs(seed: int = 0) -> dict:
    seeds = jax.random.split(jax.random.key(seed), 4)
    return {
        "points": bell_draw(seeds[0], (DIMS, NPTS), 1.0, 4.0, ((1, 512),)),
        "probes": draw_probes(jax.random.fold_in(seeds[3], 71), 0),
        "col_blocks": draw_col_blocks(jax.random.fold_in(seeds[3], 71), 0),
    }


noise_level = 3.0
half_inverse = 1.0 / 6.0


def tile_kernel(row_coords, row_norms, col_coords, col_norms):
    cross_terms = lax.dot_general(row_coords, col_coords, (((0,), (0,)), ((), ())), preferred_element_type=jnp.float32)
    distance = row_norms[:, None] + col_norms[None, :] - 2.0 * cross_terms
    return jnp.exp(-half_inverse * distance).astype(jnp.bfloat16)


def add_columns(whole, col_start, extra):
    old_block = lax.dynamic_slice_in_dim(whole, col_start, extra.shape[1], 1)
    return lax.dynamic_update_slice_in_dim(whole, old_block + extra, col_start, 1)


def reference(points, probes, col_blocks):
    coords = points.astype(jnp.float32)
    norms = jnp.sum(coords * coords, 0)
    probe_values = probes.astype(jnp.float32)
    product_out = noise_level * probe_values

    def visit_block(block_index, running):
        block_index = jnp.asarray(block_index).astype(jnp.int32)
        group_index = block_index // MEMBERS
        member_index = block_index % MEMBERS
        row_start = (block_index * P_DEV).astype(jnp.int32)
        row_coords = lax.dynamic_slice_in_dim(points, row_start, P_DEV, 1)
        row_norms = lax.dynamic_slice_in_dim(norms, row_start, P_DEV, 0)
        row_probes = lax.dynamic_slice_in_dim(probes, row_start, P_DEV, 1)
        self_tile = tile_kernel(row_coords, row_norms, row_coords, row_norms)
        running = add_columns(running, row_start, lax.dot_general(row_probes, self_tile, (((1,), (1,)), ((), ())), preferred_element_type=jnp.float32))
        partner_base = ((group_index + 1) % GROUPS) * MEMBERS

        def visit_tile(tile_step, inner):
            column = col_blocks[group_index, member_index, tile_step].astype(jnp.int32)
            col_start = ((partner_base + column) * P_DEV).astype(jnp.int32)
            col_coords = lax.dynamic_slice_in_dim(points, col_start, P_DEV, 1)
            col_norms = lax.dynamic_slice_in_dim(norms, col_start, P_DEV, 0)
            col_probes = lax.dynamic_slice_in_dim(probes, col_start, P_DEV, 1)
            kernel_block = tile_kernel(row_coords, row_norms, col_coords, col_norms)
            inner = add_columns(inner, row_start, lax.dot_general(col_probes, kernel_block, (((1,), (1,)), ((), ())), preferred_element_type=jnp.float32))
            inner = add_columns(inner, col_start, lax.dot_general(row_probes, kernel_block, (((1,), (0,)), ((), ())), preferred_element_type=jnp.float32))
            return inner

        return lax.fori_loop(0, TPD, visit_tile, running)

    product_out = lax.fori_loop(0, GROUPS * MEMBERS, visit_block, product_out)
    curvature_out = jnp.sum(probe_values * product_out, 1) / jnp.float32(NPTS)
    return product_out, curvature_out
```

```python
import functools

import jax
import jax.numpy as jnp
from jax import lax
from jax.experimental import pallas as pl
from jax.experimental.pallas import tpu as pltpu
from jax.sharding import PartitionSpec as P

MESH = pl.DeviceIdType.MESH
F32 = jnp.float32
BF16 = jnp.bfloat16

noise_level = 3.0
exponent_scale = 1.4426950408889634 / 3.0

QUAD = 4
OFFSETS = (1, -1, 2, -2, 3, -3, 4)


def split3(value):
    high = value.astype(BF16).astype(F32)
    rest = value - high
    mid = rest.astype(BF16).astype(F32)
    return high, mid, rest - mid


def fill_factor(coords, last, dest):
    pieces = coords.astype(F32)
    squares = pieces[8:16] * pieces[8:16]
    high = squares.astype(BF16).astype(F32)
    dest[0:16, :] = coords
    dest[16:32, :] = jnp.concatenate((high, squares - high), 0).astype(BF16)
    ninth = last.astype(F32)
    ninth_sq = ninth * ninth
    ninth_high = ninth_sq.astype(BF16).astype(F32)
    ninth_low = ninth_sq - ninth_high
    row = lax.broadcasted_iota(jnp.int32, (16, 128), 0)
    base = jnp.where((row >= 3) & (row < 6), 1.0, 0.0)
    for q in range(8):
        part = jnp.where(row == 0, ninth[q : q + 1], base)
        part = jnp.where(row == 1, ninth_high[q : q + 1], part)
        part = jnp.where(row == 2, ninth_low[q : q + 1], part)
        dest[32:48, q * 128 : (q + 1) * 128] = part.astype(BF16)


def kernel(
    dims, group_count, points_ref, probes_ref, listed_ref, product_ref, curvature_ref,
    panel, own, near, total, backs, outbox, inbox, row_factor, factor_a, factor_b, tile_a, tile_b,
    inverse, cur_own, cur_in, cur_group, cur_all,
    shift_sem, gather_send, gather_recv, back_send, back_recv, cur_send, cur_recv, all_send, all_recv,
):
    members, tiles, width = panel.shape[0], backs.shape[0] - 1, points_ref.shape[1]
    rows = members // QUAD
    g = lax.axis_index("group")
    m = lax.axis_index("member")
    y, quad = m // QUAD, lax.rem(m, QUAD)
    nxt = lax.rem(g + 1, group_count)
    prv = lax.rem(g + group_count - 1, group_count)
    across = y * QUAD + lax.rem(quad + 2, QUAD)
    mate = y * QUAD + quad + 1 - 2 * lax.rem(quad, 2)

    def at(row, q):
        return lax.rem(row + rows, rows) * QUAD + q

    barrier = pltpu.get_barrier_semaphore()

    def greet(group, member):
        pl.semaphore_signal(barrier, inc=1, device_id={"group": group, "member": member}, device_id_type=MESH)

    for d in OFFSETS:
        greet(g, at(y + d, quad))
    greet(g, across)
    greet(g, mate)

    def greet_group(i, _):
        greet(lax.rem(g + i, group_count), m)
        return 0

    lax.fori_loop(1, group_count, greet_group, 0)

    probe_values = probes_ref[...].astype(F32)
    coords = points_ref[...].astype(F32)
    own[:, :width] = jnp.concatenate((probe_values, coords[:8]), 0).astype(BF16)
    ninth = coords[8:9]
    folded = jnp.concatenate([ninth[:, q * 128 : (q + 1) * 128] for q in range(8)], 0)
    own[:, width:] = jnp.concatenate((folded, jnp.zeros((8, 128), F32)), 0).astype(BF16)

    pl.semaphore_wait(barrier, len(OFFSETS) + 2 + group_count - 1)

    shift = pltpu.make_async_remote_copy(
        src_ref=own, dst_ref=panel.at[m], send_sem=shift_sem, recv_sem=gather_recv.at[m],
        device_id={"group": prv, "member": m}, device_id_type=MESH,
    )
    shift.start()

    squares = coords[:8] * coords[:8]
    norm = -0.5 * (jnp.sum(squares, 0, keepdims=True) + ninth * ninth)
    norm_parts = split3(norm)
    half = jnp.full((1, width), -0.5, F32)
    side = jnp.concatenate(
        (
            jnp.zeros((8, width), F32), coords[:8], jnp.full((16, width), -0.5, F32),
            ninth, half, half, *norm_parts, jnp.zeros((128 - 38, width), F32),
        ), 0,
    )
    row_factor[...] = jnp.transpose(side)[:, :48].astype(BF16)

    backs[tiles] = jnp.zeros(backs.shape[1:], BF16)

    def find(k, _):
        place = jnp.int32(tiles)
        for t in range(tiles):
            place = jnp.where(listed_ref[0, 0, t] == k, t, place)
        inverse[k] = place
        return 0

    lax.fori_loop(0, members, find, 0)

    def exponent(factor, dest):
        dest[...] = jnp.exp2(
            exponent_scale * jnp.dot(row_factor[...], factor[...], preferred_element_type=F32)
        ).astype(BF16)

    fill_factor(own[:, :width], own[:, width:], factor_a)
    exponent(factor_a, tile_a)

    def towards_near(block, tile):
        return lax.dot_general(block, tile[...], (((1,), (1,)), ((), ())), preferred_element_type=F32)

    total[...] = noise_level * probe_values + towards_near(own[0:8, :width], tile_a)
    near[...] = jnp.zeros_like(near)

    def forward(slot, target, sem):
        copy = pltpu.make_async_remote_copy(
            src_ref=panel.at[slot], dst_ref=panel.at[slot],
            send_sem=gather_send.at[sem], recv_sem=gather_recv.at[slot],
            device_id={"group": g, "member": target}, device_id_type=MESH,
        )
        copy.start()

    def arrived(slot):
        pltpu.make_async_copy(panel.at[slot], panel.at[slot], gather_recv.at[slot]).wait()

    arrived(m)
    for i, d in enumerate(OFFSETS):
        forward(m, at(y + d, quad), i)
    lane = len(OFFSETS)
    forward(m, across, lane)
    forward(m, mate, lane + rows)
    for i, d in enumerate(OFFSETS):
        slot = at(y + d, quad)
        arrived(slot)
        forward(slot, across, lane + 1 + i)
        forward(slot, mate, lane + rows + 1 + i)
    far = lax.rem(quad + 2, QUAD)
    for i, d in enumerate((0,) + OFFSETS):
        slot = at(y + d, far)
        arrived(slot)
        forward(slot, mate, lane + 2 * rows + i)
    sibling = quad + 1 - 2 * lax.rem(quad, 2)
    for q in (sibling, lax.rem(sibling + 2, QUAD)):
        for d in (0,) + OFFSETS:
            arrived(at(y + d, q))

    def prepare(t, factor):
        k = listed_ref[0, 0, t]
        block = panel[k]
        fill_factor(block[:, :width], block[:, width:], factor)

    half_width = width // 2

    def products(t, tile):
        k = listed_ref[0, 0, t]
        near[...] += towards_near(panel[k, 0:8, :width], tile)
        back = jnp.dot(own[0:8, :width], tile[...], preferred_element_type=F32)
        backs[t] = jnp.concatenate((back[:, :half_width], back[:, half_width:]), 0).astype(BF16)

    prepare(0, factor_a)
    exponent(factor_a, tile_a)
    prepare(1, factor_b)

    def pair(u, _):
        products(2 * u, tile_a)
        exponent(factor_b, tile_b)
        prepare(2 * u + 2, factor_a)
        products(2 * u + 1, tile_b)
        exponent(factor_a, tile_a)
        prepare(2 * u + 3, factor_b)
        return 0

    lax.fori_loop(0, tiles // 2 - 1, pair, 0)
    products(tiles - 2, tile_a)
    exponent(factor_b, tile_b)
    products(tiles - 1, tile_b)

    weighted = probe_values * (total[...] + 2.0 * near[...])
    local = weighted[:, :128]
    for q in range(1, width // 128):
        local = local + weighted[:, q * 128 : (q + 1) * 128]
    cur_own[...] = local

    def cur_copy(i):
        peer = lax.rem(m + i, members)
        return pltpu.make_async_remote_copy(
            src_ref=cur_own, dst_ref=cur_in.at[i], send_sem=cur_send.at[i], recv_sem=cur_recv.at[i],
            device_id={"group": g, "member": peer}, device_id_type=MESH,
        )

    def all_copy(i):
        return pltpu.make_async_remote_copy(
            src_ref=cur_group, dst_ref=cur_all.at[i], send_sem=all_send.at[i], recv_sem=all_recv.at[i],
            device_id={"group": lax.rem(g + i, group_count), "member": m}, device_id_type=MESH,
        )

    def back_copy(k):
        return pltpu.make_async_remote_copy(
            src_ref=outbox.at[k], dst_ref=inbox.at[m], send_sem=back_send.at[k], recv_sem=back_recv.at[m],
            device_id={"group": nxt, "member": k}, device_id_type=MESH,
        )

    def each(first, last, step):
        def body(i, _):
            step(i)
            return 0

        lax.fori_loop(first, last, body, 0)

    each(1, members, lambda i: cur_copy(i).start())

    def give_back(i):
        k = lax.rem(m + i, members)
        outbox[k] = backs[inverse[k]]
        back_copy(k).start()

    each(0, members, give_back)

    each(1, members, lambda i: cur_copy(i).wait_recv())
    cur_group[...] = lax.fori_loop(1, members, lambda i, s: s + cur_in[i], cur_own[...])
    each(1, group_count, lambda i: all_copy(i).start())

    def returned(i, state):
        k = lax.rem(m - i + members, members)
        pltpu.make_async_copy(inbox.at[k], inbox.at[k], back_recv.at[k]).wait()
        return state + inbox[k].astype(F32)

    share = lax.fori_loop(0, members, returned, jnp.zeros(inbox.shape[1:], F32))
    product_ref[...] = total[...] + near[...] + jnp.concatenate((share[:8], share[8:]), 1)

    each(1, group_count, lambda i: all_copy(i).wait_recv())
    whole = lax.fori_loop(1, group_count, lambda i, s: s + cur_all[i], cur_group[...])
    curvature_ref[...] = jnp.sum(whole, 1, keepdims=True) * (1.0 / (width * members * group_count))

    shift.wait_send()

    def sent(i):
        pltpu.make_async_copy(panel.at[0], panel.at[0], gather_send.at[i]).wait()

    each(0, len(OFFSETS) + 3 * rows, sent)
    each(0, members, lambda k: back_copy(k).wait_send())
    each(1, members, lambda i: cur_copy(i).wait_send())
    each(1, group_count, lambda i: all_copy(i).wait_send())


def body(points, probes, col_blocks):
    width, dims, rhs = points.shape[1], points.shape[0], probes.shape[0]
    members, groups, tiles = lax.axis_size("member"), lax.axis_size("group"), col_blocks.shape[2]
    rows = members // QUAD
    vmem = pl.BlockSpec(memory_space=pltpu.VMEM)
    dma = pltpu.SemaphoreType.DMA
    product, curvature = pl.pallas_call(
        functools.partial(kernel, dims, groups),
        out_shape=(jax.ShapeDtypeStruct((rhs, width), F32), jax.ShapeDtypeStruct((rhs, 1), F32)),
        in_specs=[vmem, vmem, pl.BlockSpec(memory_space=pltpu.SMEM)],
        out_specs=(vmem, vmem),
        scratch_shapes=[
            pltpu.VMEM((members, 16, width + 128), BF16),
            pltpu.VMEM((16, width + 128), BF16),
            pltpu.VMEM((rhs, width), F32),
            pltpu.VMEM((rhs, width), F32),
            pltpu.VMEM((tiles + 1, 16, width // 2), BF16),
            pltpu.VMEM((members, 16, width // 2), BF16),
            pltpu.VMEM((members, 16, width // 2), BF16),
            pltpu.VMEM((width, 48), BF16),
            pltpu.VMEM((48, width), BF16),
            pltpu.VMEM((48, width), BF16),
            pltpu.VMEM((width, width), BF16),
            pltpu.VMEM((width, width), BF16),
            pltpu.SMEM((members,), jnp.int32),
            pltpu.VMEM((rhs, 128), F32),
            pltpu.VMEM((members, rhs, 128), F32),
            pltpu.VMEM((rhs, 128), F32),
            pltpu.VMEM((groups, rhs, 128), F32),
            dma, dma((len(OFFSETS) + 3 * rows,)), dma((members,)),
            dma((members,)), dma((members,)),
            dma((members,)), dma((members,)),
            dma((groups,)), dma((groups,)),
        ],
        compiler_params=pltpu.CompilerParams(
            collective_id=0, has_side_effects=True, vmem_limit_bytes=40 * 2**20
        ),
    )(points, probes, col_blocks)
    return product, curvature[:, 0]


def solution(mesh):
    return jax.shard_map(
        body,
        mesh=mesh,
        in_specs=(
            P(None, ("group", "member")),
            P(None, ("group", "member")),
            P("group", "member", None),
        ),
        out_specs=(P(None, ("group", "member")), P()),
        check_vma=False,
    )
```

```python
import functools

import jax
import jax.numpy as jnp
from jax import lax
from jax.experimental import pallas as pl
from jax.experimental.pallas import tpu as pltpu
from jax.sharding import PartitionSpec as P

MESH = pl.DeviceIdType.MESH
F32 = jnp.float32
BF16 = jnp.bfloat16

noise_level = 3.0
exponent_scale = 1.4426950408889634 / 3.0

QUAD = 4
ORDER = (0, 1, -1, 3, -3, 2, -2, 4)
NEAR = 5


def split3(value):
    high = value.astype(BF16).astype(F32)
    rest = value - high
    mid = rest.astype(BF16).astype(F32)
    return high, mid, rest - mid


def fill_factor(coords, last, dest):
    pieces = coords.astype(F32)
    squares = pieces[8:16] * pieces[8:16]
    high = squares.astype(BF16).astype(F32)
    dest[0:16, :] = coords
    dest[16:32, :] = jnp.concatenate((high, squares - high), 0).astype(BF16)
    ninth = last.astype(F32)
    ninth_sq = ninth * ninth
    ninth_high = ninth_sq.astype(BF16).astype(F32)
    ninth_low = ninth_sq - ninth_high
    row = lax.broadcasted_iota(jnp.int32, (16, 128), 0)
    base = jnp.where((row >= 3) & (row < 6), 1.0, 0.0)
    for q in range(8):
        part = jnp.where(row == 0, ninth[q : q + 1], base)
        part = jnp.where(row == 1, ninth_high[q : q + 1], part)
        part = jnp.where(row == 2, ninth_low[q : q + 1], part)
        dest[32:48, q * 128 : (q + 1) * 128] = part.astype(BF16)


def kernel(
    dims, group_count, points_ref, probes_ref, listed_ref, product_ref, curvature_ref,
    near_panel, far_panel, own, near, total, backs, outbox, inbox, row_factor, factor_a, factor_b, tile_a, tile_b,
    inverse, sequence, cur_own, cur_in, cur_group, cur_all,
    met, gather_send, gather_recv, back_send, back_recv, cur_send, cur_recv, all_send, all_recv,
):
    members, tiles, width = outbox.shape[0], backs.shape[0] - 1, points_ref.shape[1]
    rows = members // QUAD
    close = NEAR * QUAD
    g = lax.axis_index("group")
    m = lax.axis_index("member")
    y, quad = m // QUAD, lax.rem(m, QUAD)
    nxt = lax.rem(g + 1, group_count)
    prv = lax.rem(g + group_count - 1, group_count)
    across = y * QUAD + lax.rem(quad + 2, QUAD)
    mate = y * QUAD + quad + 1 - 2 * lax.rem(quad, 2)

    def at(row, q):
        return lax.rem(row + rows, rows) * QUAD + q

    barrier = pltpu.get_barrier_semaphore()

    def greet(group, member):
        pl.semaphore_signal(barrier, inc=1, device_id={"group": group, "member": member}, device_id_type=MESH)

    greet(nxt, m)
    for d in ORDER[1:]:
        greet(g, at(y + d, quad))
    greet(g, across)
    greet(g, mate)

    probe_values = probes_ref[...].astype(F32)
    coords = points_ref[...].astype(F32)
    own[:, :width] = jnp.concatenate((probe_values, coords[:8]), 0).astype(BF16)
    ninth = coords[8:9]
    folded = jnp.concatenate([ninth[:, q * 128 : (q + 1) * 128] for q in range(8)], 0)
    own[:, width:] = jnp.concatenate((folded, jnp.zeros((8, 128), F32)), 0).astype(BF16)

    across_quad = lax.rem(quad + 2, QUAD)
    mate_quad = quad + 1 - 2 * lax.rem(quad, 2)

    def spot(place, q):
        if place < NEAR:
            return near_panel.at[place * QUAD + q]
        return far_panel.at[(place - NEAR) * QUAD + q]

    shift = pltpu.make_async_remote_copy(
        src_ref=own, dst_ref=spot(0, quad), send_sem=gather_send.at[0], recv_sem=gather_recv.at[quad],
        device_id={"group": prv, "member": m}, device_id_type=MESH,
    )

    def passing(place, q, to_place, to, sem):
        return pltpu.make_async_remote_copy(
            src_ref=spot(place, q), dst_ref=spot(to_place, q),
            send_sem=gather_send.at[sem], recv_sem=gather_recv.at[to_place * QUAD + q],
            device_id={"group": g, "member": to}, device_id_type=MESH,
        )

    def along(place):
        d = ORDER[place]
        seen = place if d == rows // 2 else ORDER.index(-d)
        return passing(0, quad, seen, at(y + d, quad), place)

    def over(place):
        return passing(place, quad, place, across, rows + place)

    def aside(place):
        return passing(place, quad, place, mate, 2 * rows + place)

    def aside_across(place):
        return passing(place, across_quad, place, mate, 3 * rows + place)

    def arrived(place, q):
        passing(place, q, place, mate, 0).wait_recv()

    pl.semaphore_wait(barrier, rows + 2)
    shift.start()

    squares = coords[:8] * coords[:8]
    norm = -0.5 * (jnp.sum(squares, 0, keepdims=True) + ninth * ninth)
    norm_parts = split3(norm)
    half = jnp.full((1, width), -0.5, F32)
    side = jnp.concatenate(
        (
            jnp.zeros((8, width), F32), coords[:8], jnp.full((16, width), -0.5, F32),
            ninth, half, half, *norm_parts, jnp.zeros((128 - 38, width), F32),
        ), 0,
    )
    row_factor[...] = jnp.transpose(side)[:, :48].astype(BF16)

    backs[tiles] = jnp.zeros(backs.shape[1:], BF16)

    def member_at(position):
        place = position // QUAD
        d = jnp.int32(ORDER[0])
        for i in range(1, rows):
            d = jnp.where(place == i, ORDER[i], d)
        return at(y + d, lax.rem(position, QUAD))

    def find(position, count):
        k = member_at(position)
        hit = jnp.int32(0)
        for t in range(tiles):
            hit = jnp.where(listed_ref[0, 0, t] == k, 1, hit)
        inverse[position] = jnp.where(hit == 1, count, tiles)
        return count + hit

    lax.fori_loop(0, members, find, jnp.int32(0))

    def order(t, _):
        position = jnp.int32(0)
        for p in range(members):
            position = jnp.where(inverse[p] == t, p, position)
        sequence[t] = position
        return 0

    lax.fori_loop(0, tiles, order, 0)

    def exponent(factor, dest):
        dest[...] = jnp.exp2(
            exponent_scale * jnp.dot(row_factor[...], factor[...], preferred_element_type=F32)
        ).astype(BF16)

    fill_factor(own[:, :width], own[:, width:], factor_a)
    exponent(factor_a, tile_a)

    def towards_near(block, tile):
        return lax.dot_general(block, tile[...], (((1,), (1,)), ((), ())), preferred_element_type=F32)

    total[...] = noise_level * probe_values + towards_near(own[0:8, :width], tile_a)
    near[...] = jnp.zeros_like(near)

    def spread(places):
        for place in places:
            along(place).start()

    def relay(places):
        for place in places:
            if place > 0:
                arrived(place, quad)
            over(place).start()
            aside(place).start()

    def relay_across(places):
        for place in places:
            arrived(place, across_quad)
            aside_across(place).start()

    def settle(places):
        for place in places:
            arrived(place, mate_quad)
            arrived(place, lax.rem(mate_quad + 2, QUAD))

    arrived(0, quad)
    spread(range(1, NEAR))
    relay(range(NEAR))
    relay_across(range(NEAR))
    settle(range(NEAR))

    def meet(step):
        for group in (g + (1 << step), g + group_count - (1 << step)):
            pl.semaphore_signal(
                met.at[step], inc=1, device_id={"group": lax.rem(group, group_count), "member": m}, device_id_type=MESH
            )

    meet(0)
    spread(range(NEAR, rows))

    def block_near(t):
        return near_panel[jnp.minimum(sequence[t], close - 1)]

    def block_any(t):
        position = sequence[t]
        a = near_panel[jnp.minimum(position, close - 1)]
        b = far_panel[jnp.maximum(position - close, 0)]
        return jnp.where(position < close, a, b)

    def prepare(block, factor):
        fill_factor(block[:, :width], block[:, width:], factor)

    half_width = width // 2

    def add_near(factor, tile):
        near[...] += towards_near(factor[0:8, :], tile)

    def keep_back(t, tile):
        back = jnp.dot(own[0:8, :width], tile[...], preferred_element_type=F32)
        backs[t] = jnp.concatenate((back[:, :half_width], back[:, half_width:]), 0).astype(BF16)

    def products(t, factor, tile):
        add_near(factor, tile)
        keep_back(t, tile)

    def back_copy(position):
        return pltpu.make_async_remote_copy(
            src_ref=outbox.at[position], dst_ref=inbox.at[m],
            send_sem=back_send.at[position], recv_sem=back_recv.at[m],
            device_id={"group": nxt, "member": member_at(position)}, device_id_type=MESH,
        )

    def give_back(position):
        outbox[position] = backs[inverse[position]]
        back_copy(position).start()

    prepare(block_near(0), factor_a)
    exponent(factor_a, tile_a)
    prepare(block_near(1), factor_b)

    def pair(u, block):
        products(2 * u, factor_a, tile_a)
        exponent(factor_b, tile_b)
        prepare(block(2 * u + 2), factor_a)
        products(2 * u + 1, factor_b, tile_b)
        exponent(factor_a, tile_a)
        prepare(block(2 * u + 3), factor_b)
        give_back(2 * u)
        give_back(2 * u + 1)

    early = 3

    def early_pair(u, _):
        pair(u, block_near)
        for step, acts in enumerate(((), (relay,), (relay_across, settle))):

            @pl.when(u == step)
            def _(step=step, acts=acts):
                for act in acts:
                    act(range(NEAR, rows))
                pl.semaphore_wait(met.at[step], 2)
                if step < 2:
                    meet(step + 1)

        return 0

    def late_pair(u, _):
        pair(u, block_any)
        return 0

    lax.fori_loop(0, early, early_pair, 0)
    lax.fori_loop(early, tiles // 2 - 1, late_pair, 0)
    add_near(factor_a, tile_a)
    exponent(factor_b, tile_b)
    add_near(factor_b, tile_b)

    weighted = probe_values * (total[...] + 2.0 * near[...])
    local = weighted[:, :128]
    for q in range(1, width // 128):
        local = local + weighted[:, q * 128 : (q + 1) * 128]
    line = lax.broadcasted_iota(jnp.int32, local.shape, 0)
    lane = lax.broadcasted_iota(jnp.int32, local.shape, 1)
    sums = jnp.where(line == lane, jnp.sum(local, 1, keepdims=True), 0.0)
    cur_own[...] = jnp.sum(sums, 0, keepdims=True)
    cur_in[0] = cur_own[...]

    def cur_copy(i):
        peer = lax.rem(m + i, members)
        return pltpu.make_async_remote_copy(
            src_ref=cur_own, dst_ref=cur_in.at[i], send_sem=cur_send.at[i], recv_sem=cur_recv.at[i],
            device_id={"group": g, "member": peer}, device_id_type=MESH,
        )

    def all_copy(i):
        return pltpu.make_async_remote_copy(
            src_ref=cur_group, dst_ref=cur_all.at[i], send_sem=all_send.at[i], recv_sem=all_recv.at[i],
            device_id={"group": lax.rem(g + i, group_count), "member": m}, device_id_type=MESH,
        )

    def each(first, last, step):
        def body(i, _):
            step(i)
            return 0

        lax.fori_loop(first, last, body, 0)

    each(1, members, lambda i: cur_copy(i).start())

    keep_back(tiles - 2, tile_a)
    keep_back(tiles - 1, tile_b)
    each(tiles - 2, members, give_back)

    each(1, members, lambda i: cur_copy(i).wait_recv())
    cur_group[...] = jnp.sum(cur_in[...], 0)
    cur_all[0] = cur_group[...]
    each(1, group_count, lambda i: all_copy(i).start())

    def returned(i, state):
        k = lax.rem(m - i + members, members)
        pltpu.make_async_copy(inbox.at[k], inbox.at[k], back_recv.at[k]).wait()
        return state + inbox[k].astype(F32)

    share = lax.fori_loop(0, members, returned, jnp.zeros(inbox.shape[1:], F32))
    product_ref[...] = total[...] + near[...] + jnp.concatenate((share[:8], share[8:]), 1)

    each(1, group_count, lambda i: all_copy(i).wait_recv())
    curvature_ref[...] = jnp.sum(cur_all[...], 0) * (1.0 / (width * members * group_count))

    for place in range(rows):
        (along(place) if place else shift).wait_send()
        over(place).wait_send()
        aside(place).wait_send()
        aside_across(place).wait_send()
    each(0, members, lambda p: back_copy(p).wait_send())
    each(1, members, lambda i: cur_copy(i).wait_send())
    each(1, group_count, lambda i: all_copy(i).wait_send())


def body(points, probes, col_blocks):
    width, dims, rhs = points.shape[1], points.shape[0], probes.shape[0]
    members, groups, tiles = lax.axis_size("member"), lax.axis_size("group"), col_blocks.shape[2]
    rows = members // QUAD
    vmem = pl.BlockSpec(memory_space=pltpu.VMEM)
    dma = pltpu.SemaphoreType.DMA
    product, curvature = pl.pallas_call(
        functools.partial(kernel, dims, groups),
        out_shape=(jax.ShapeDtypeStruct((rhs, width), F32), jax.ShapeDtypeStruct((1, 128), F32)),
        in_specs=[vmem, vmem, pl.BlockSpec(memory_space=pltpu.SMEM)],
        out_specs=(vmem, vmem),
        scratch_shapes=[
            pltpu.VMEM((NEAR * QUAD, 16, width + 128), BF16),
            pltpu.VMEM((members - NEAR * QUAD, 16, width + 128), BF16),
            pltpu.VMEM((16, width + 128), BF16),
            pltpu.VMEM((rhs, width), F32),
            pltpu.VMEM((rhs, width), F32),
            pltpu.VMEM((tiles + 1, 16, width // 2), BF16),
            pltpu.VMEM((members, 16, width // 2), BF16),
            pltpu.VMEM((members, 16, width // 2), BF16),
            pltpu.VMEM((width, 48), BF16),
            pltpu.VMEM((48, width), BF16),
            pltpu.VMEM((48, width), BF16),
            pltpu.VMEM((width, width), BF16),
            pltpu.VMEM((width, width), BF16),
            pltpu.SMEM((members,), jnp.int32),
            pltpu.SMEM((tiles,), jnp.int32),
            pltpu.VMEM((1, 128), F32),
            pltpu.VMEM((members, 1, 128), F32),
            pltpu.VMEM((1, 128), F32),
            pltpu.VMEM((groups, 1, 128), F32),
            pltpu.SemaphoreType.REGULAR((3,)), dma((4 * rows,)), dma((members,)),
            dma((members,)), dma((members,)),
            dma((members,)), dma((members,)),
            dma((groups,)), dma((groups,)),
        ],
        compiler_params=pltpu.CompilerParams(
            collective_id=0, has_side_effects=True, vmem_limit_bytes=40 * 2**20
        ),
    )(points, probes, col_blocks)
    return product, curvature[0, :rhs]


def solution(mesh):
    return jax.shard_map(
        body,
        mesh=mesh,
        in_specs=(
            P(None, ("group", "member")),
            P(None, ("group", "member")),
            P("group", "member", None),
        ),
        out_specs=(P(None, ("group", "member")), P()),
        check_vma=False,
    )
```

```python
import functools

import jax
import jax.numpy as jnp
from jax import lax
from jax.experimental import pallas as pl
from jax.experimental.pallas import tpu as pltpu
from jax.sharding import PartitionSpec as P

MESH = pl.DeviceIdType.MESH
F32 = jnp.float32
BF16 = jnp.bfloat16

noise_level = 3.0
exponent_scale = 1.4426950408889634 / 3.0

QUAD = 4
ORDER = (0, 2, -2, 3, -3, 1, -1, 4)
HOME = ORDER.index(0)
NEAR = 5


def split3(value):
    high = value.astype(BF16).astype(F32)
    rest = value - high
    mid = rest.astype(BF16).astype(F32)
    return high, mid, rest - mid


def fill_factor(coords, last, dest):
    pieces = coords.astype(F32)
    squares = pieces[8:16] * pieces[8:16]
    high = squares.astype(BF16).astype(F32)
    dest[0:16, :] = coords
    dest[16:32, :] = jnp.concatenate((high, squares - high), 0).astype(BF16)
    ninth = last.astype(F32)
    ninth_sq = ninth * ninth
    ninth_high = ninth_sq.astype(BF16).astype(F32)
    ninth_low = ninth_sq - ninth_high
    row = lax.broadcasted_iota(jnp.int32, (16, 128), 0)
    base = jnp.where((row >= 3) & (row < 6), 1.0, 0.0)
    for q in range(8):
        part = jnp.where(row == 0, ninth[q : q + 1], base)
        part = jnp.where(row == 1, ninth_high[q : q + 1], part)
        part = jnp.where(row == 2, ninth_low[q : q + 1], part)
        dest[32:48, q * 128 : (q + 1) * 128] = part.astype(BF16)


def kernel(
    dims, group_count, points_ref, probes_ref, listed_ref, product_ref, curvature_ref,
    near_panel, far_panel, own, near, total, backs, outbox, inbox, row_factor, factor_a, factor_b, tile_a, tile_b,
    inverse, sequence, cur_own, cur_in, cur_group, cur_all,
    met, gather_send, gather_recv, back_send, back_recv, cur_send, cur_recv, all_send, all_recv,
):
    members, tiles, width = outbox.shape[0], backs.shape[0] - 1, points_ref.shape[1]
    rows = members // QUAD
    close = NEAR * QUAD
    g = lax.axis_index("group")
    m = lax.axis_index("member")
    y, quad = m // QUAD, lax.rem(m, QUAD)
    nxt = lax.rem(g + 1, group_count)
    prv = lax.rem(g + group_count - 1, group_count)
    across = y * QUAD + lax.rem(quad + 2, QUAD)
    mate = y * QUAD + quad + 1 - 2 * lax.rem(quad, 2)

    def at(row, q):
        return lax.rem(row + rows, rows) * QUAD + q

    barrier = pltpu.get_barrier_semaphore()

    def greet(group, member):
        pl.semaphore_signal(barrier, inc=1, device_id={"group": group, "member": member}, device_id_type=MESH)

    greet(nxt, m)
    for d in ORDER:
        if d != 0:
            greet(g, at(y + d, quad))
    greet(g, across)
    greet(g, mate)

    probe_values = probes_ref[...].astype(F32)
    coords = points_ref[...].astype(F32)
    own[:, :width] = jnp.concatenate((probe_values, coords[:8]), 0).astype(BF16)
    ninth = coords[8:9]
    folded = jnp.concatenate([ninth[:, q * 128 : (q + 1) * 128] for q in range(8)], 0)
    own[:, width:] = jnp.concatenate((folded, jnp.zeros((8, 128), F32)), 0).astype(BF16)

    across_quad = lax.rem(quad + 2, QUAD)
    mate_quad = quad + 1 - 2 * lax.rem(quad, 2)

    def spot(place, q):
        if place < NEAR:
            return near_panel.at[place * QUAD + q]
        return far_panel.at[(place - NEAR) * QUAD + q]

    shift = pltpu.make_async_remote_copy(
        src_ref=own, dst_ref=spot(HOME, quad), send_sem=gather_send.at[0], recv_sem=gather_recv.at[HOME * QUAD + quad],
        device_id={"group": prv, "member": m}, device_id_type=MESH,
    )

    def passing(place, q, to_place, to, sent_with):
        return pltpu.make_async_remote_copy(
            src_ref=spot(place, q), dst_ref=spot(to_place, q),
            send_sem=gather_send.at[0 if sent_with < NEAR else 1], recv_sem=gather_recv.at[to_place * QUAD + q],
            device_id={"group": g, "member": to}, device_id_type=MESH,
        )

    def along(place):
        d = ORDER[place]
        seen = place if d == rows // 2 else ORDER.index(-d)
        return passing(HOME, quad, seen, at(y + d, quad), place)

    def over(place):
        return passing(place, quad, place, across, place)

    def aside(place):
        return passing(place, quad, place, mate, place)

    def aside_across(place):
        return passing(place, across_quad, place, mate, place)

    def arrived(place, q):
        passing(place, q, place, mate, 0).wait_recv()

    pl.semaphore_wait(barrier, rows + 2)
    shift.start()

    squares = coords[:8] * coords[:8]
    norm = -0.5 * (jnp.sum(squares, 0, keepdims=True) + ninth * ninth)
    norm_parts = split3(norm)
    half = jnp.full((1, width), -0.5, F32)
    side = jnp.concatenate(
        (
            jnp.zeros((8, width), F32), coords[:8], jnp.full((16, width), -0.5, F32),
            ninth, half, half, *norm_parts, jnp.zeros((128 - 38, width), F32),
        ), 0,
    )
    row_factor[...] = jnp.transpose(side)[:, :48].astype(BF16)

    def exponent(factor, dest):
        dest[...] = jnp.exp2(
            exponent_scale * jnp.dot(row_factor[...], factor[...], preferred_element_type=F32)
        ).astype(BF16)

    def spread(places):
        for place in places:
            if place != HOME:
                along(place).start()

    def relay(places):
        for place in places:
            if place != HOME:
                arrived(place, quad)
            over(place).start()
            aside(place).start()

    def relay_across(places):
        for place in places:
            arrived(place, across_quad)
            aside_across(place).start()

    def settle(places):
        for place in places:
            arrived(place, mate_quad)
            arrived(place, lax.rem(mate_quad + 2, QUAD))

    arrived(HOME, quad)
    spread(range(NEAR))
    relay((HOME,))

    backs[tiles] = jnp.zeros(backs.shape[1:], BF16)

    def member_at(position):
        place = position // QUAD
        d = jnp.int32(ORDER[0])
        for i in range(1, rows):
            d = jnp.where(place == i, ORDER[i], d)
        return at(y + d, lax.rem(position, QUAD))

    def find(position, count):
        k = member_at(position)
        hit = jnp.int32(0)
        for t in range(tiles):
            hit = jnp.where(listed_ref[0, 0, t] == k, 1, hit)
        inverse[position] = jnp.where(hit == 1, count, tiles)
        return count + hit

    lax.fori_loop(0, members, find, jnp.int32(0))

    def order(t, _):
        position = jnp.int32(0)
        for p in range(members):
            position = jnp.where(inverse[p] == t, p, position)
        sequence[t] = position
        return 0

    lax.fori_loop(0, tiles, order, 0)

    relay([place for place in range(NEAR) if place != HOME])

    fill_factor(own[:, :width], own[:, width:], factor_a)
    exponent(factor_a, tile_a)

    def towards_near(block, tile):
        return lax.dot_general(block, tile[...], (((1,), (1,)), ((), ())), preferred_element_type=F32)

    total[...] = noise_level * probe_values + towards_near(own[0:8, :width], tile_a)
    near[...] = jnp.zeros_like(near)

    relay_across(range(NEAR))
    settle(range(NEAR))

    def meet(step):
        for group in (g + (1 << step), g + group_count - (1 << step)):
            pl.semaphore_signal(
                met.at[step], inc=1, device_id={"group": lax.rem(group, group_count), "member": m}, device_id_type=MESH
            )

    meet(0)
    spread(range(NEAR, rows))

    def block_near(t):
        return near_panel[jnp.minimum(sequence[t], close - 1)]

    def block_any(t):
        position = sequence[t]
        a = near_panel[jnp.minimum(position, close - 1)]
        b = far_panel[jnp.maximum(position - close, 0)]
        return jnp.where(position < close, a, b)

    def prepare(block, factor):
        fill_factor(block[:, :width], block[:, width:], factor)

    half_width = width // 2

    def add_near(block, tile):
        near[...] += towards_near(block, tile)

    def keep_back(t, tile):
        back = jnp.dot(own[0:8, :width], tile[...], preferred_element_type=F32)
        backs[t] = jnp.concatenate((back[:, :half_width], back[:, half_width:]), 0).astype(BF16)

    def products(t, factor, tile):
        add_near(factor[0:8, :], tile)
        keep_back(t, tile)

    def back_copy(position):
        return pltpu.make_async_remote_copy(
            src_ref=outbox.at[position], dst_ref=inbox.at[m],
            send_sem=back_send, recv_sem=back_recv,
            device_id={"group": nxt, "member": member_at(position)}, device_id_type=MESH,
        )

    def give_back(position):
        outbox[position] = backs[inverse[position]]
        back_copy(position).start()

    prepare(block_near(0), factor_a)
    exponent(factor_a, tile_a)
    prepare(block_near(1), factor_b)

    def pair(u, block):
        products(2 * u, factor_a, tile_a)
        exponent(factor_b, tile_b)
        prepare(block(2 * u + 2), factor_a)
        products(2 * u + 1, factor_b, tile_b)
        exponent(factor_a, tile_a)
        prepare(block(2 * u + 3), factor_b)
        give_back(2 * u)
        give_back(2 * u + 1)

    early = 3

    def early_pair(u, _):
        pair(u, block_near)
        for step, acts in enumerate(((), (relay,), (relay_across, settle))):

            @pl.when(u == step)
            def _(step=step, acts=acts):
                for act in acts:
                    act([place for place in range(NEAR, rows) if act != relay or place != HOME])
                pl.semaphore_wait(met.at[step], 2)
                if step < 2:
                    meet(step + 1)

        return 0

    def late_pair(u, _):
        pair(u, block_any)
        return 0

    lax.fori_loop(0, early, early_pair, 0)
    lax.fori_loop(early, tiles // 2 - 1, late_pair, 0)
    add_near(factor_a[0:8, :], tile_a)
    exponent(factor_b, tile_b)
    add_near(factor_b[0:8, :], tile_b)

    weighted = probe_values * (total[...] + 2.0 * near[...])
    local = weighted[:, :128]
    for q in range(1, width // 128):
        local = local + weighted[:, q * 128 : (q + 1) * 128]
    line = lax.broadcasted_iota(jnp.int32, local.shape, 0)
    lane = lax.broadcasted_iota(jnp.int32, local.shape, 1)
    sums = jnp.where(line == lane, jnp.sum(local, 1, keepdims=True), 0.0)
    cur_own[...] = jnp.sum(sums, 0, keepdims=True)
    cur_in[0] = cur_own[...]

    def cur_copy(i):
        peer = lax.rem(m + i, members)
        return pltpu.make_async_remote_copy(
            src_ref=cur_own, dst_ref=cur_in.at[i], send_sem=cur_send, recv_sem=cur_recv,
            device_id={"group": g, "member": peer}, device_id_type=MESH,
        )

    def all_copy(i):
        return pltpu.make_async_remote_copy(
            src_ref=cur_group, dst_ref=cur_all.at[i], send_sem=all_send, recv_sem=all_recv,
            device_id={"group": lax.rem(g + i, group_count), "member": m}, device_id_type=MESH,
        )

    def each(first, last, step):
        def body(i, _):
            step(i)
            return 0

        lax.fori_loop(first, last, body, 0)

    each(1, members, lambda i: cur_copy(i).start())

    keep_back(tiles - 2, tile_a)
    keep_back(tiles - 1, tile_b)
    each(tiles - 2, members, lambda i: give_back(members - 1 + tiles - 2 - i))


    def whole(ref, send_sem, recv_sem):
        return pltpu.make_async_remote_copy(
            src_ref=ref, dst_ref=ref, send_sem=send_sem, recv_sem=recv_sem,
            device_id={"group": g, "member": mate}, device_id_type=MESH,
        )

    rest = pl.ds(1, members - 1)
    whole(cur_in.at[rest], cur_send, cur_recv).wait_recv()
    cur_group[...] = jnp.sum(cur_in[...], 0)
    cur_all[0] = cur_group[...]
    each(1, group_count, lambda i: all_copy(i).start())

    whole(near_panel, gather_send.at[0], gather_recv.at[0]).wait_send()
    whole(far_panel, gather_send.at[1], gather_recv.at[0]).wait_send()
    whole(cur_in.at[rest], cur_send, cur_recv).wait_send()
    whole(outbox, back_send, back_recv).wait_send()
    others = cur_all.at[pl.ds(1, group_count - 1)]
    whole(others, all_send, all_recv).wait_send()

    whole(inbox, back_send, back_recv).wait_recv()
    share = inbox[0].astype(F32)
    for k in range(1, members):
        share = share + inbox[k].astype(F32)
    product_ref[...] = total[...] + near[...] + jnp.concatenate((share[:8], share[8:]), 1)

    whole(others, all_send, all_recv).wait_recv()
    curvature_ref[...] = jnp.sum(cur_all[...], 0) * (1.0 / (width * members * group_count))


def body(points, probes, col_blocks):
    width, dims, rhs = points.shape[1], points.shape[0], probes.shape[0]
    members, groups, tiles = lax.axis_size("member"), lax.axis_size("group"), col_blocks.shape[2]
    rows = members // QUAD
    vmem = pl.BlockSpec(memory_space=pltpu.VMEM)
    dma = pltpu.SemaphoreType.DMA
    product, curvature = pl.pallas_call(
        functools.partial(kernel, dims, groups),
        out_shape=(jax.ShapeDtypeStruct((rhs, width), F32), jax.ShapeDtypeStruct((1, 128), F32)),
        in_specs=[vmem, vmem, pl.BlockSpec(memory_space=pltpu.SMEM)],
        out_specs=(vmem, vmem),
        scratch_shapes=[
            pltpu.VMEM((NEAR * QUAD, 16, width + 128), BF16),
            pltpu.VMEM((members - NEAR * QUAD, 16, width + 128), BF16),
            pltpu.VMEM((16, width + 128), BF16),
            pltpu.VMEM((rhs, width), F32),
            pltpu.VMEM((rhs, width), F32),
            pltpu.VMEM((tiles + 1, 16, width // 2), BF16),
            pltpu.VMEM((members, 16, width // 2), BF16),
            pltpu.VMEM((members, 16, width // 2), BF16),
            pltpu.VMEM((width, 48), BF16),
            pltpu.VMEM((48, width), BF16),
            pltpu.VMEM((48, width), BF16),
            *[pltpu.VMEM((width, width), BF16)] * 2,
            pltpu.SMEM((members,), jnp.int32),
            pltpu.SMEM((tiles,), jnp.int32),
            pltpu.VMEM((1, 128), F32),
            pltpu.VMEM((members, 1, 128), F32),
            pltpu.VMEM((1, 128), F32),
            pltpu.VMEM((groups, 1, 128), F32),
            pltpu.SemaphoreType.REGULAR((3,)), dma((2,)), dma((members,)),
            dma, dma, dma, dma, dma, dma,
        ],
        compiler_params=pltpu.CompilerParams(
            collective_id=0, has_side_effects=True, vmem_limit_bytes=48 * 2**20
        ),
    )(points, probes, col_blocks)
    return product, curvature[0, :rhs]


def solution(mesh):
    return jax.shard_map(
        body,
        mesh=mesh,
        in_specs=(
            P(None, ("group", "member")),
            P(None, ("group", "member")),
            P("group", "member", None),
        ),
        out_specs=(P(None, ("group", "member")), P()),
        check_vma=False,
    )
```

```python
import functools

import jax
import jax.numpy as jnp
from jax import lax
from jax.experimental import pallas as pl
from jax.experimental.pallas import tpu as pltpu
from jax.sharding import PartitionSpec as P

MESH = pl.DeviceIdType.MESH
F32 = jnp.float32
BF16 = jnp.bfloat16

noise_level = 3.0
exponent_scale = 1.4426950408889634 / 3.0

QUAD = 4
ORDER = (2, -2, 3, -3, 0, 1, -1, 4)
HOME = ORDER.index(0)
SINGLE = 4
NEAR = 5


def split3(value):
    high = value.astype(BF16).astype(F32)
    rest = value - high
    mid = rest.astype(BF16).astype(F32)
    return high, mid, rest - mid


def fill_factor(coords, last, dest):
    pieces = coords.astype(F32)
    squares = pieces[8:16] * pieces[8:16]
    high = squares.astype(BF16).astype(F32)
    dest[0:16, :] = coords
    dest[16:32, :] = jnp.concatenate((high, squares - high), 0).astype(BF16)
    ninth = last.astype(F32)
    ninth_sq = ninth * ninth
    ninth_high = ninth_sq.astype(BF16).astype(F32)
    ninth_low = ninth_sq - ninth_high
    row = lax.broadcasted_iota(jnp.int32, (16, 128), 0)
    base = jnp.where((row >= 3) & (row < 6), 1.0, 0.0)
    for q in range(8):
        part = jnp.where(row == 0, ninth[q : q + 1], base)
        part = jnp.where(row == 1, ninth_high[q : q + 1], part)
        part = jnp.where(row == 2, ninth_low[q : q + 1], part)
        dest[32:48, q * 128 : (q + 1) * 128] = part.astype(BF16)


def kernel(
    dims, group_count, points_ref, probes_ref, listed_ref, product_ref, curvature_ref,
    near_panel, far_panel, own, near, total, backs, outbox, inbox, mate_out, mate_in, row_factor, factor_a, factor_b, tile_a, tile_b,
    inverse, sequence, cur_own, cur_in, cur_group, cur_all,
    met, gather_send, gather_recv, back_send, back_recv, cur_send, cur_recv, all_send, all_recv, mate_send, mate_recv,
):
    tiles, width = backs.shape[0] - 1, points_ref.shape[1]
    members = lax.axis_size("member")
    rows = members // QUAD
    close = NEAR * QUAD
    single = SINGLE * QUAD
    g = lax.axis_index("group")
    m = lax.axis_index("member")
    y, quad = m // QUAD, lax.rem(m, QUAD)
    nxt = lax.rem(g + 1, group_count)
    prv = lax.rem(g + group_count - 1, group_count)
    across = y * QUAD + lax.rem(quad + 2, QUAD)
    mate = y * QUAD + quad + 1 - 2 * lax.rem(quad, 2)

    def at(row, q):
        return lax.rem(row + rows, rows) * QUAD + q

    barrier = pltpu.get_barrier_semaphore()

    def greet(group, member):
        pl.semaphore_signal(barrier, inc=1, device_id={"group": group, "member": member}, device_id_type=MESH)

    greet(nxt, m)
    for d in ORDER:
        if d != 0:
            greet(g, at(y + d, quad))
    greet(g, across)
    greet(g, mate)

    probe_values = probes_ref[...].astype(F32)
    coords = points_ref[...].astype(F32)
    own[:, :width] = jnp.concatenate((probe_values, coords[:8]), 0).astype(BF16)
    ninth = coords[8:9]
    folded = jnp.concatenate([ninth[:, q * 128 : (q + 1) * 128] for q in range(8)], 0)
    own[:, width:] = jnp.concatenate((folded, jnp.zeros((8, 128), F32)), 0).astype(BF16)

    across_quad = lax.rem(quad + 2, QUAD)
    mate_quad = quad + 1 - 2 * lax.rem(quad, 2)

    def spot(place, q):
        if place < NEAR:
            return near_panel.at[place * QUAD + q]
        return far_panel.at[(place - NEAR) * QUAD + q]

    shift = pltpu.make_async_remote_copy(
        src_ref=own, dst_ref=spot(HOME, quad), send_sem=gather_send.at[0], recv_sem=gather_recv.at[HOME * QUAD + quad],
        device_id={"group": prv, "member": m}, device_id_type=MESH,
    )

    def passing(place, q, to_place, to, sent_with):
        return pltpu.make_async_remote_copy(
            src_ref=spot(place, q), dst_ref=spot(to_place, q),
            send_sem=gather_send.at[0 if sent_with < NEAR else 1], recv_sem=gather_recv.at[to_place * QUAD + q],
            device_id={"group": g, "member": to}, device_id_type=MESH,
        )

    def along(place):
        d = ORDER[place]
        seen = place if d == rows // 2 else ORDER.index(-d)
        return passing(HOME, quad, seen, at(y + d, quad), place)

    def over(place):
        return passing(place, quad, place, across, place)

    def aside(place):
        return passing(place, quad, place, mate, place)

    def aside_across(place):
        return passing(place, across_quad, place, mate, place)

    def arrived(place, q):
        passing(place, q, place, mate, 0).wait_recv()

    pl.semaphore_wait(barrier, rows + 2)
    shift.start()

    squares = coords[:8] * coords[:8]
    norm = -0.5 * (jnp.sum(squares, 0, keepdims=True) + ninth * ninth)
    norm_parts = split3(norm)
    half = jnp.full((1, width), -0.5, F32)
    side = jnp.concatenate(
        (
            jnp.zeros((8, width), F32), coords[:8], jnp.full((16, width), -0.5, F32),
            ninth, half, half, *norm_parts, jnp.zeros((128 - 38, width), F32),
        ), 0,
    )
    row_factor[...] = jnp.transpose(side)[:, :48].astype(BF16)

    def exponent(factor, dest):
        dest[...] = jnp.exp2(
            exponent_scale * jnp.dot(row_factor[...], factor[...], preferred_element_type=F32)
        ).astype(BF16)

    def spread(places):
        for place in places:
            if place != HOME:
                along(place).start()

    def relay(places):
        for place in places:
            if place != HOME:
                arrived(place, quad)
            over(place).start()
            aside(place).start()

    def relay_across(places):
        for place in places:
            arrived(place, across_quad)
            aside_across(place).start()

    def settle(places):
        for place in places:
            arrived(place, mate_quad)
            arrived(place, lax.rem(mate_quad + 2, QUAD))

    arrived(HOME, quad)
    spread(range(NEAR))
    relay((HOME,))

    backs[tiles] = jnp.zeros(backs.shape[1:], BF16)

    def member_at(position):
        place = position // QUAD
        d = jnp.int32(ORDER[0])
        for i in range(1, rows):
            d = jnp.where(place == i, ORDER[i], d)
        return at(y + d, lax.rem(position, QUAD))

    def find(position, count):
        k = member_at(position)
        hit = jnp.int32(0)
        for t in range(tiles):
            hit = jnp.where(listed_ref[0, 0, t] == k, 1, hit)
        inverse[position] = jnp.where(hit == 1, count, tiles)
        return count + hit

    lax.fori_loop(0, members, find, jnp.int32(0))

    def order(t, _):
        position = jnp.int32(0)
        for p in range(members):
            position = jnp.where(inverse[p] == t, p, position)
        sequence[t] = position
        return 0

    lax.fori_loop(0, tiles, order, 0)

    relay([place for place in range(NEAR) if place != HOME])

    fill_factor(own[:, :width], own[:, width:], factor_a)
    exponent(factor_a, tile_a)

    def towards_near(block, tile):
        return lax.dot_general(block, tile[...], (((1,), (1,)), ((), ())), preferred_element_type=F32)

    total[...] = noise_level * probe_values + towards_near(own[0:8, :width], tile_a)
    near[...] = jnp.zeros_like(near)

    relay_across(range(NEAR))
    settle(range(NEAR))

    def meet(step):
        for group in (g + (1 << step), g + group_count - (1 << step)):
            pl.semaphore_signal(
                met.at[step], inc=1, device_id={"group": lax.rem(group, group_count), "member": m}, device_id_type=MESH
            )

    meet(0)
    spread(range(NEAR, rows))

    def block_near(t):
        return near_panel[jnp.minimum(sequence[t], close - 1)]

    def block_any(t):
        position = sequence[t]
        a = near_panel[jnp.minimum(position, close - 1)]
        b = far_panel[jnp.maximum(position - close, 0)]
        return jnp.where(position < close, a, b)

    def prepare(block, factor):
        fill_factor(block[:, :width], block[:, width:], factor)

    half_width = width // 2

    def add_near(block, tile):
        near[...] += towards_near(block, tile)

    def keep_back(t, tile):
        back = jnp.dot(own[0:8, :width], tile[...], preferred_element_type=F32)
        backs[t] = jnp.concatenate((back[:, :half_width], back[:, half_width:]), 0).astype(BF16)

    def products(t, factor, tile):
        add_near(factor[0:8, :], tile)
        keep_back(t, tile)

    def back_copy(position, box, slot):
        return pltpu.make_async_remote_copy(
            src_ref=outbox.at[box], dst_ref=inbox.at[slot], send_sem=back_send, recv_sem=back_recv,
            device_id={"group": nxt, "member": member_at(position)}, device_id_type=MESH,
        )

    def give_back(position):
        outbox[position] = backs[inverse[position]]
        back_copy(position, position, position // QUAD * QUAD + quad).start()

    prepare(block_near(0), factor_a)
    exponent(factor_a, tile_a)
    prepare(block_near(1), factor_b)

    def pair(u, block):
        products(2 * u, factor_a, tile_a)
        exponent(factor_b, tile_b)
        prepare(block(2 * u + 2), factor_a)
        products(2 * u + 1, factor_b, tile_b)
        exponent(factor_a, tile_a)
        prepare(block(2 * u + 3), factor_b)

        @pl.when(2 * u < single)
        def _():
            give_back(2 * u)
            give_back(2 * u + 1)


    early = 3

    def early_pair(u, _):
        pair(u, block_near)
        for step, acts in enumerate(((), (relay,), (relay_across, settle))):

            @pl.when(u == step)
            def _(step=step, acts=acts):
                for act in acts:
                    act([place for place in range(NEAR, rows) if act != relay or place != HOME])
                pl.semaphore_wait(met.at[step], 2)
                if step < 2:
                    meet(step + 1)

        return 0

    def late_pair(u, _):
        pair(u, block_any)
        return 0

    lax.fori_loop(0, early, early_pair, 0)
    lax.fori_loop(early, tiles // 2 - 1, late_pair, 0)
    add_near(factor_a[0:8, :], tile_a)
    exponent(factor_b, tile_b)
    add_near(factor_b[0:8, :], tile_b)

    weighted = probe_values * (total[...] + 2.0 * near[...])
    local = weighted[:, :128]
    for q in range(1, width // 128):
        local = local + weighted[:, q * 128 : (q + 1) * 128]
    line = lax.broadcasted_iota(jnp.int32, local.shape, 0)
    lane = lax.broadcasted_iota(jnp.int32, local.shape, 1)
    sums = jnp.where(line == lane, jnp.sum(local, 1, keepdims=True), 0.0)
    cur_own[...] = jnp.sum(sums, 0, keepdims=True)
    cur_in[0] = cur_own[...]

    def cur_copy(i):
        peer = lax.rem(m + i, members)
        return pltpu.make_async_remote_copy(
            src_ref=cur_own, dst_ref=cur_in.at[i], send_sem=cur_send, recv_sem=cur_recv,
            device_id={"group": g, "member": peer}, device_id_type=MESH,
        )

    def all_copy(i):
        return pltpu.make_async_remote_copy(
            src_ref=cur_group, dst_ref=cur_all.at[i], send_sem=all_send, recv_sem=all_recv,
            device_id={"group": lax.rem(g + i, group_count), "member": m}, device_id_type=MESH,
        )

    def each(first, last, step):
        def body(i, _):
            step(i)
            return 0

        lax.fori_loop(first, last, body, 0)

    def whole(ref, send_sem, recv_sem):
        return pltpu.make_async_remote_copy(
            src_ref=ref, dst_ref=ref, send_sem=send_sem, recv_sem=recv_sem,
            device_id={"group": g, "member": mate}, device_id_type=MESH,
        )

    each(1, members, lambda i: cur_copy(i).start())

    keep_back(tiles - 2, tile_a)
    keep_back(tiles - 1, tile_b)

    core = lax.rem(quad, 2)
    shared = (members - single) // 2

    def hand_over(j):
        mate_out[j] = backs[inverse[single + 2 * j + 1 - core]]
        pltpu.make_async_remote_copy(
            src_ref=mate_out.at[j], dst_ref=mate_in.at[j], send_sem=mate_send, recv_sem=mate_recv,
            device_id={"group": g, "member": mate}, device_id_type=MESH,
        ).start()

    def give_sum(i):
        j = shared - 1 - i
        position = single + 2 * j + core
        sums = backs[inverse[position]].astype(F32) + mate_in[j].astype(F32)
        outbox[single + j] = sums.astype(BF16)
        back_copy(position, single + j, single + j // 2 * 2 + quad // 2).start()

    each(0, shared, hand_over)
    whole(mate_in, mate_send, mate_recv).wait_recv()
    each(0, shared, give_sum)


    rest = pl.ds(1, members - 1)
    whole(cur_in.at[rest], cur_send, cur_recv).wait_recv()
    cur_group[...] = jnp.sum(cur_in[...], 0)
    cur_all[0] = cur_group[...]
    each(1, group_count, lambda i: all_copy(i).start())

    whole(near_panel, gather_send.at[0], gather_recv.at[0]).wait_send()
    whole(far_panel, gather_send.at[1], gather_recv.at[0]).wait_send()
    whole(cur_in.at[rest], cur_send, cur_recv).wait_send()
    whole(mate_out, mate_send, mate_recv).wait_send()
    whole(outbox, back_send, back_recv).wait_send()
    others = cur_all.at[pl.ds(1, group_count - 1)]
    whole(others, all_send, all_recv).wait_send()

    whole(inbox, back_send, back_recv).wait_recv()
    share = inbox[0].astype(F32)
    for k in range(1, inbox.shape[0]):
        share = share + inbox[k].astype(F32)
    product_ref[...] = total[...] + near[...] + jnp.concatenate((share[:8], share[8:]), 1)

    whole(others, all_send, all_recv).wait_recv()
    curvature_ref[...] = jnp.sum(cur_all[...], 0) * (1.0 / (width * members * group_count))


def body(points, probes, col_blocks):
    width, dims, rhs = points.shape[1], points.shape[0], probes.shape[0]
    members, groups, tiles = lax.axis_size("member"), lax.axis_size("group"), col_blocks.shape[2]
    rows = members // QUAD
    boxes = (members + SINGLE * QUAD) // 2
    vmem = pl.BlockSpec(memory_space=pltpu.VMEM)
    dma = pltpu.SemaphoreType.DMA
    product, curvature = pl.pallas_call(
        functools.partial(kernel, dims, groups),
        out_shape=(jax.ShapeDtypeStruct((rhs, width), F32), jax.ShapeDtypeStruct((1, 128), F32)),
        in_specs=[vmem, vmem, pl.BlockSpec(memory_space=pltpu.SMEM)],
        out_specs=(vmem, vmem),
        scratch_shapes=[
            pltpu.VMEM((NEAR * QUAD, 16, width + 128), BF16),
            pltpu.VMEM((members - NEAR * QUAD, 16, width + 128), BF16),
            pltpu.VMEM((16, width + 128), BF16),
            pltpu.VMEM((rhs, width), F32),
            pltpu.VMEM((rhs, width), F32),
            pltpu.VMEM((tiles + 1, 16, width // 2), BF16),
            *[pltpu.VMEM((boxes, 16, width // 2), BF16)] * 2,
            *[pltpu.VMEM(((members - SINGLE * QUAD) // 2, 16, width // 2), BF16)] * 2,
            pltpu.VMEM((width, 48), BF16),
            pltpu.VMEM((48, width), BF16),
            pltpu.VMEM((48, width), BF16),
            *[pltpu.VMEM((width, width), BF16)] * 2,
            pltpu.SMEM((members,), jnp.int32),
            pltpu.SMEM((tiles,), jnp.int32),
            pltpu.VMEM((1, 128), F32),
            pltpu.VMEM((members, 1, 128), F32),
            pltpu.VMEM((1, 128), F32),
            pltpu.VMEM((groups, 1, 128), F32),
            pltpu.SemaphoreType.REGULAR((3,)), dma((2,)), dma((members,)),
            *[dma] * 8,
        ],
        compiler_params=pltpu.CompilerParams(
            collective_id=0, has_side_effects=True, vmem_limit_bytes=48 * 2**20
        ),
    )(points, probes, col_blocks)
    return product, curvature[0, :rhs]


def solution(mesh):
    return jax.shard_map(
        body,
        mesh=mesh,
        in_specs=(
            P(None, ("group", "member")),
            P(None, ("group", "member")),
            P("group", "member", None),
        ),
        out_specs=(P(None, ("group", "member")), P()),
        check_vma=False,
    )
```

```python
import functools

import jax
import jax.numpy as jnp
from jax import lax
from jax.experimental import pallas as pl
from jax.experimental.pallas import tpu as pltpu
from jax.sharding import PartitionSpec as P

MESH = pl.DeviceIdType.MESH
F32 = jnp.float32
BF16 = jnp.bfloat16

noise_level = 3.0
exponent_scale = 1.4426950408889634 / 3.0

QUAD = 4
ORDER = (1, -1, 3, -3, 0, 2, -2, 4)
HOME = ORDER.index(0)
SINGLE = 4
NEAR = 5


def split3(value):
    high = value.astype(BF16).astype(F32)
    rest = value - high
    mid = rest.astype(BF16).astype(F32)
    return high, mid, rest - mid


def fill_factor(coords, last, dest):
    pieces = coords.astype(F32)
    squares = pieces[8:16] * pieces[8:16]
    high = squares.astype(BF16).astype(F32)
    dest[0:16, :] = coords
    dest[16:32, :] = jnp.concatenate((high, squares - high), 0).astype(BF16)
    ninth = last.astype(F32)
    ninth_sq = ninth * ninth
    ninth_high = ninth_sq.astype(BF16).astype(F32)
    ninth_low = ninth_sq - ninth_high
    row = lax.broadcasted_iota(jnp.int32, (16, 128), 0)
    base = jnp.where((row >= 3) & (row < 6), 1.0, 0.0)
    for q in range(8):
        part = jnp.where(row == 0, ninth[q : q + 1], base)
        part = jnp.where(row == 1, ninth_high[q : q + 1], part)
        part = jnp.where(row == 2, ninth_low[q : q + 1], part)
        dest[32:48, q * 128 : (q + 1) * 128] = part.astype(BF16)


def kernel(
    dims, group_count, points_ref, probes_ref, listed_ref, product_ref, curvature_ref,
    near_panel, far_panel, own, near, total, backs, outbox, inbox, mate_out, mate_in, row_factor, factor_a, factor_b, tile_a, tile_b,
    inverse, sequence, cur_own, cur_in, cur_group, cur_all,
    met, gather_send, gather_recv, back_send, back_recv, cur_send, cur_recv, all_send, all_recv, mate_send, mate_recv,
):
    tiles, width = backs.shape[0] - 1, points_ref.shape[1]
    members = lax.axis_size("member")
    rows = members // QUAD
    close = NEAR * QUAD
    single = SINGLE * QUAD
    g = lax.axis_index("group")
    m = lax.axis_index("member")
    y, quad = m // QUAD, lax.rem(m, QUAD)
    nxt = lax.rem(g + 1, group_count)
    prv = lax.rem(g + group_count - 1, group_count)
    across = y * QUAD + lax.rem(quad + 2, QUAD)
    mate = y * QUAD + quad + 1 - 2 * lax.rem(quad, 2)

    def at(row, q):
        return lax.rem(row + rows, rows) * QUAD + q

    barrier = pltpu.get_barrier_semaphore()

    def greet(group, member):
        pl.semaphore_signal(barrier, inc=1, device_id={"group": group, "member": member}, device_id_type=MESH)

    greet(nxt, m)
    for d in ORDER:
        if d != 0:
            greet(g, at(y + d, quad))
    greet(g, across)
    greet(g, mate)

    probe_values = probes_ref[...].astype(F32)
    coords = points_ref[...].astype(F32)
    own[:, :width] = jnp.concatenate((probe_values, coords[:8]), 0).astype(BF16)
    ninth = coords[8:9]
    folded = jnp.concatenate([ninth[:, q * 128 : (q + 1) * 128] for q in range(8)], 0)
    own[:, width:] = jnp.concatenate((folded, jnp.zeros((8, 128), F32)), 0).astype(BF16)

    across_quad = lax.rem(quad + 2, QUAD)
    mate_quad = quad + 1 - 2 * lax.rem(quad, 2)

    def spot(place, q):
        if place < NEAR:
            return near_panel.at[place * QUAD + q]
        return far_panel.at[(place - NEAR) * QUAD + q]

    shift = pltpu.make_async_remote_copy(
        src_ref=own, dst_ref=spot(HOME, quad), send_sem=gather_send.at[0], recv_sem=gather_recv.at[HOME * QUAD + quad],
        device_id={"group": prv, "member": m}, device_id_type=MESH,
    )

    def passing(place, q, to_place, to, sent_with):
        return pltpu.make_async_remote_copy(
            src_ref=spot(place, q), dst_ref=spot(to_place, q),
            send_sem=gather_send.at[0 if sent_with < NEAR else 1], recv_sem=gather_recv.at[to_place * QUAD + q],
            device_id={"group": g, "member": to}, device_id_type=MESH,
        )

    def along(place):
        d = ORDER[place]
        seen = place if d == rows // 2 else ORDER.index(-d)
        return passing(HOME, quad, seen, at(y + d, quad), place)

    def over(place):
        return passing(place, quad, place, across, place)

    def aside(place):
        return passing(place, quad, place, mate, place)

    def aside_across(place):
        return passing(place, across_quad, place, mate, place)

    def arrived(place, q):
        passing(place, q, place, mate, 0).wait_recv()

    pl.semaphore_wait(barrier, rows + 2)
    shift.start()

    squares = coords[:8] * coords[:8]
    norm = -0.5 * (jnp.sum(squares, 0, keepdims=True) + ninth * ninth)
    norm_parts = split3(norm)
    half = jnp.full((1, width), -0.5, F32)
    side = jnp.concatenate(
        (
            jnp.zeros((8, width), F32), coords[:8], jnp.full((16, width), -0.5, F32),
            ninth, half, half, *norm_parts, jnp.zeros((128 - 38, width), F32),
        ), 0,
    )
    row_factor[...] = jnp.transpose(side)[:, :48].astype(BF16)

    def exponent(factor, dest):
        dest[...] = jnp.exp2(
            exponent_scale * jnp.dot(row_factor[...], factor[...], preferred_element_type=F32)
        ).astype(BF16)

    def spread(places):
        for place in places:
            if place != HOME:
                along(place).start()

    def relay(places):
        for place in places:
            if place != HOME:
                arrived(place, quad)
            over(place).start()
            aside(place).start()

    def relay_across(places):
        for place in places:
            arrived(place, across_quad)
            aside_across(place).start()

    def settle(places):
        for place in places:
            arrived(place, mate_quad)
            arrived(place, lax.rem(mate_quad + 2, QUAD))

    arrived(HOME, quad)
    spread(range(NEAR))
    relay((HOME,))

    backs[tiles] = jnp.zeros(backs.shape[1:], BF16)

    def member_at(position):
        place = position // QUAD
        d = jnp.int32(ORDER[0])
        for i in range(1, rows):
            d = jnp.where(place == i, ORDER[i], d)
        return at(y + d, lax.rem(position, QUAD))

    def find(position, count):
        k = member_at(position)
        hit = jnp.int32(0)
        for t in range(tiles):
            hit = jnp.where(listed_ref[0, 0, t] == k, 1, hit)
        inverse[position] = jnp.where(hit == 1, count, tiles)
        return count + hit

    lax.fori_loop(0, members, find, jnp.int32(0))

    def order(t, _):
        position = jnp.int32(0)
        for p in range(members):
            position = jnp.where(inverse[p] == t, p, position)
        sequence[t] = position
        return 0

    lax.fori_loop(0, tiles, order, 0)

    relay([place for place in range(NEAR) if place != HOME])

    fill_factor(own[:, :width], own[:, width:], factor_a)
    exponent(factor_a, tile_a)

    def towards_near(block, tile):
        return lax.dot_general(block, tile[...], (((1,), (1,)), ((), ())), preferred_element_type=F32)

    total[...] = noise_level * probe_values + towards_near(own[0:8, :width], tile_a)
    near[...] = jnp.zeros_like(near)

    relay_across(range(NEAR))
    settle(range(NEAR))

    def meet(step):
        for group in (g + (1 << step), g + group_count - (1 << step)):
            pl.semaphore_signal(
                met.at[step], inc=1, device_id={"group": lax.rem(group, group_count), "member": m}, device_id_type=MESH
            )

    meet(0)
    spread(range(NEAR, rows))

    def block_near(t):
        return near_panel[jnp.minimum(sequence[t], close - 1)]

    def block_any(t):
        position = sequence[t]
        a = near_panel[jnp.minimum(position, close - 1)]
        b = far_panel[jnp.maximum(position - close, 0)]
        return jnp.where(position < close, a, b)

    def prepare(block, factor):
        fill_factor(block[:, :width], block[:, width:], factor)

    half_width = width // 2

    def add_near(block, tile):
        near[...] += towards_near(block, tile)

    def keep_back(t, tile):
        back = jnp.dot(own[0:8, :width], tile[...], preferred_element_type=F32)
        backs[t] = jnp.concatenate((back[:, :half_width], back[:, half_width:]), 0).astype(BF16)

    def products(t, factor, tile):
        add_near(factor[0:8, :], tile)
        keep_back(t, tile)

    def back_copy(position, box, slot):
        return pltpu.make_async_remote_copy(
            src_ref=outbox.at[box], dst_ref=inbox.at[slot], send_sem=back_send, recv_sem=back_recv,
            device_id={"group": nxt, "member": member_at(position)}, device_id_type=MESH,
        )

    def give_back(position):
        outbox[position] = backs[inverse[position]]
        back_copy(position, position, position // QUAD * QUAD + quad).start()

    prepare(block_near(0), factor_a)
    exponent(factor_a, tile_a)
    prepare(block_near(1), factor_b)

    def pair(u, block):
        products(2 * u, factor_a, tile_a)
        exponent(factor_b, tile_b)
        prepare(block(2 * u + 2), factor_a)
        products(2 * u + 1, factor_b, tile_b)
        exponent(factor_a, tile_a)
        prepare(block(2 * u + 3), factor_b)

        @pl.when(2 * u < single)
        def _():
            give_back(2 * u)
            give_back(2 * u + 1)


    early = 3

    def early_pair(u, _):
        pair(u, block_near)
        for step, acts in enumerate(((), (relay,), (relay_across, settle))):

            @pl.when(u == step)
            def _(step=step, acts=acts):
                for act in acts:
                    act([place for place in range(NEAR, rows) if act != relay or place != HOME])
                pl.semaphore_wait(met.at[step], 2)
                if step < 2:
                    meet(step + 1)

        return 0

    def late_pair(u, _):
        pair(u, block_any)
        return 0

    lax.fori_loop(0, early, early_pair, 0)
    lax.fori_loop(early, tiles // 2 - 1, late_pair, 0)
    products(tiles - 2, factor_a, tile_a)
    exponent(factor_b, tile_b)
    add_near(factor_b[0:8, :], tile_b)

    weighted = probe_values * (total[...] + 2.0 * near[...])
    local = weighted[:, :128]
    for q in range(1, width // 128):
        local = local + weighted[:, q * 128 : (q + 1) * 128]
    line = lax.broadcasted_iota(jnp.int32, local.shape, 0)
    lane = lax.broadcasted_iota(jnp.int32, local.shape, 1)
    sums = jnp.where(line == lane, jnp.sum(local, 1, keepdims=True), 0.0)
    cur_own[...] = jnp.sum(sums, 0, keepdims=True)
    cur_in[0] = cur_own[...]

    def cur_copy(i):
        peer = lax.rem(m + i, members)
        return pltpu.make_async_remote_copy(
            src_ref=cur_own, dst_ref=cur_in.at[i], send_sem=cur_send, recv_sem=cur_recv,
            device_id={"group": g, "member": peer}, device_id_type=MESH,
        )

    def all_copy(i):
        return pltpu.make_async_remote_copy(
            src_ref=cur_group, dst_ref=cur_all.at[i], send_sem=all_send, recv_sem=all_recv,
            device_id={"group": lax.rem(g + i, group_count), "member": m}, device_id_type=MESH,
        )

    def each(first, last, step):
        def body(i, _):
            step(i)
            return 0

        lax.fori_loop(first, last, body, 0)

    def whole(ref, send_sem, recv_sem):
        return pltpu.make_async_remote_copy(
            src_ref=ref, dst_ref=ref, send_sem=send_sem, recv_sem=recv_sem,
            device_id={"group": g, "member": mate}, device_id_type=MESH,
        )

    each(1, members, lambda i: cur_copy(i).start())

    keep_back(tiles - 1, tile_b)

    core = lax.rem(quad, 2)
    shared = (members - single) // 2

    def hand_over(j):
        mate_out[j] = backs[inverse[single + 2 * j + 1 - core]]
        pltpu.make_async_remote_copy(
            src_ref=mate_out.at[j], dst_ref=mate_in.at[j], send_sem=mate_send, recv_sem=mate_recv,
            device_id={"group": g, "member": mate}, device_id_type=MESH,
        ).start()

    def give_sum(i):
        j = shared - 1 - i
        position = single + 2 * j + core
        sums = backs[inverse[position]].astype(F32) + mate_in[j].astype(F32)
        outbox[single + j] = sums.astype(BF16)
        back_copy(position, single + j, single + j // 2 * 2 + quad // 2).start()

    each(0, shared, hand_over)
    whole(mate_in, mate_send, mate_recv).wait_recv()
    each(0, shared, give_sum)


    rest = pl.ds(1, members - 1)
    whole(cur_in.at[rest], cur_send, cur_recv).wait_recv()
    cur_group[...] = jnp.sum(cur_in[...], 0)
    cur_all[0] = cur_group[...]
    each(1, group_count, lambda i: all_copy(i).start())

    whole(near_panel, gather_send.at[0], gather_recv.at[0]).wait_send()
    whole(far_panel, gather_send.at[1], gather_recv.at[0]).wait_send()
    whole(cur_in.at[rest], cur_send, cur_recv).wait_send()
    whole(mate_out, mate_send, mate_recv).wait_send()
    whole(outbox, back_send, back_recv).wait_send()
    others = cur_all.at[pl.ds(1, group_count - 1)]
    whole(others, all_send, all_recv).wait_send()

    whole(inbox, back_send, back_recv).wait_recv()
    share = inbox[0].astype(F32)
    for k in range(1, inbox.shape[0]):
        share = share + inbox[k].astype(F32)
    product_ref[...] = total[...] + near[...] + jnp.concatenate((share[:8], share[8:]), 1)

    whole(others, all_send, all_recv).wait_recv()
    curvature_ref[...] = jnp.sum(cur_all[...], 0) * (1.0 / (width * members * group_count))


def body(points, probes, col_blocks):
    width, dims, rhs = points.shape[1], points.shape[0], probes.shape[0]
    members, groups, tiles = lax.axis_size("member"), lax.axis_size("group"), col_blocks.shape[2]
    rows = members // QUAD
    boxes = (members + SINGLE * QUAD) // 2
    vmem = pl.BlockSpec(memory_space=pltpu.VMEM)
    dma = pltpu.SemaphoreType.DMA
    product, curvature = pl.pallas_call(
        functools.partial(kernel, dims, groups),
        out_shape=(jax.ShapeDtypeStruct((rhs, width), F32), jax.ShapeDtypeStruct((1, 128), F32)),
        in_specs=[vmem, vmem, pl.BlockSpec(memory_space=pltpu.SMEM)],
        out_specs=(vmem, vmem),
        scratch_shapes=[
            pltpu.VMEM((NEAR * QUAD, 16, width + 128), BF16),
            pltpu.VMEM((members - NEAR * QUAD, 16, width + 128), BF16),
            pltpu.VMEM((16, width + 128), BF16),
            pltpu.VMEM((rhs, width), F32),
            pltpu.VMEM((rhs, width), F32),
            pltpu.VMEM((tiles + 1, 16, width // 2), BF16),
            *[pltpu.VMEM((boxes, 16, width // 2), BF16)] * 2,
            *[pltpu.VMEM(((members - SINGLE * QUAD) // 2, 16, width // 2), BF16)] * 2,
            pltpu.VMEM((width, 48), BF16),
            pltpu.VMEM((48, width), BF16),
            pltpu.VMEM((48, width), BF16),
            *[pltpu.VMEM((width, width), BF16)] * 2,
            pltpu.SMEM((members,), jnp.int32),
            pltpu.SMEM((tiles,), jnp.int32),
            pltpu.VMEM((1, 128), F32),
            pltpu.VMEM((members, 1, 128), F32),
            pltpu.VMEM((1, 128), F32),
            pltpu.VMEM((groups, 1, 128), F32),
            pltpu.SemaphoreType.REGULAR((3,)), dma((2,)), dma((members,)),
            *[dma] * 8,
        ],
        compiler_params=pltpu.CompilerParams(
            collective_id=0, has_side_effects=True, vmem_limit_bytes=48 * 2**20
        ),
    )(points, probes, col_blocks)
    return product, curvature[0, :rhs]


def solution(mesh):
    return jax.shard_map(
        body,
        mesh=mesh,
        in_specs=(
            P(None, ("group", "member")),
            P(None, ("group", "member")),
            P("group", "member", None),
        ),
        out_specs=(P(None, ("group", "member")), P()),
        check_vma=False,
    )
```

```python
import functools

import jax
import jax.numpy as jnp
from jax import lax
from jax.experimental import pallas as pl
from jax.experimental.pallas import tpu as pltpu
from jax.sharding import PartitionSpec as P

MESH = pl.DeviceIdType.MESH
F32 = jnp.float32
BF16 = jnp.bfloat16

noise_level = 3.0
exponent_scale = 1.4426950408889634 / 3.0

QUAD = 4
ORDER = (1, -1, 3, -3, 0, 2, -2, 4)
HOME = ORDER.index(0)
SINGLE = 4
NEAR = 5


def split3(value):
    high = value.astype(BF16).astype(F32)
    rest = value - high
    mid = rest.astype(BF16).astype(F32)
    return high, mid, rest - mid


def fill_factor(coords, last, dest):
    pieces = coords.astype(F32)
    squares = pieces[8:16] * pieces[8:16]
    high = squares.astype(BF16).astype(F32)
    dest[0:16, :] = coords
    dest[16:32, :] = jnp.concatenate((high, squares - high), 0).astype(BF16)
    ninth = last.astype(F32)
    ninth_sq = ninth * ninth
    ninth_high = ninth_sq.astype(BF16).astype(F32)
    ninth_low = ninth_sq - ninth_high
    row = lax.broadcasted_iota(jnp.int32, (16, 128), 0)
    base = jnp.where((row >= 3) & (row < 6), 1.0, 0.0)
    for q in range(8):
        part = jnp.where(row == 0, ninth[q : q + 1], base)
        part = jnp.where(row == 1, ninth_high[q : q + 1], part)
        part = jnp.where(row == 2, ninth_low[q : q + 1], part)
        dest[32:48, q * 128 : (q + 1) * 128] = part.astype(BF16)


def kernel(
    dims, group_count, points_ref, probes_ref, listed_ref, product_ref, curvature_ref,
    near_panel, far_panel, own, near, total, backs, outbox, inbox, mate_out, mate_in, row_factor, factor_a, factor_b, tile_a, tile_b,
    inverse, sequence, cur_own, cur_in, cur_group, cur_all,
    met, gather_send, gather_recv, back_send, back_recv, cur_send, cur_recv, all_send, all_recv, mate_send, mate_recv,
):
    tiles, width = backs.shape[0] - 1, points_ref.shape[1]
    members = lax.axis_size("member")
    rows = members // QUAD
    close = NEAR * QUAD
    single = SINGLE * QUAD
    g = lax.axis_index("group")
    m = lax.axis_index("member")
    y, quad = m // QUAD, lax.rem(m, QUAD)
    nxt = lax.rem(g + 1, group_count)
    prv = lax.rem(g + group_count - 1, group_count)
    across = y * QUAD + lax.rem(quad + 2, QUAD)
    mate = y * QUAD + quad + 1 - 2 * lax.rem(quad, 2)

    def at(row, q):
        return lax.rem(row + rows, rows) * QUAD + q

    barrier = pltpu.get_barrier_semaphore()

    def greet(group, member):
        pl.semaphore_signal(barrier, inc=1, device_id={"group": group, "member": member}, device_id_type=MESH)

    greet(nxt, m)
    for d in ORDER:
        if d != 0:
            greet(g, at(y + d, quad))
    greet(g, across)
    greet(g, mate)

    probe_values = probes_ref[...].astype(F32)
    coords = points_ref[...].astype(F32)
    own[:, :width] = jnp.concatenate((probe_values, coords[:8]), 0).astype(BF16)
    ninth = coords[8:9]
    folded = jnp.concatenate([ninth[:, q * 128 : (q + 1) * 128] for q in range(8)], 0)
    own[:, width:] = jnp.concatenate((folded, jnp.zeros((8, 128), F32)), 0).astype(BF16)

    across_quad = lax.rem(quad + 2, QUAD)
    mate_quad = quad + 1 - 2 * lax.rem(quad, 2)

    def spot(place, q):
        if place < NEAR:
            return near_panel.at[place * QUAD + q]
        return far_panel.at[(place - NEAR) * QUAD + q]

    shift = pltpu.make_async_remote_copy(
        src_ref=own, dst_ref=spot(HOME, quad), send_sem=gather_send.at[0], recv_sem=gather_recv.at[HOME * QUAD + quad],
        device_id={"group": prv, "member": m}, device_id_type=MESH,
    )

    def passing(place, q, to_place, to, sent_with):
        return pltpu.make_async_remote_copy(
            src_ref=spot(place, q), dst_ref=spot(to_place, q),
            send_sem=gather_send.at[0 if sent_with < NEAR else 1], recv_sem=gather_recv.at[to_place * QUAD + q],
            device_id={"group": g, "member": to}, device_id_type=MESH,
        )

    def along(place):
        d = ORDER[place]
        seen = place if d == rows // 2 else ORDER.index(-d)
        return passing(HOME, quad, seen, at(y + d, quad), place)

    def over(place):
        return passing(place, quad, place, across, place)

    def aside(place):
        return passing(place, quad, place, mate, place)

    def aside_across(place):
        return passing(place, across_quad, place, mate, place)

    def arrived(place, q):
        passing(place, q, place, mate, 0).wait_recv()

    pl.semaphore_wait(barrier, rows + 2)
    shift.start()

    squares = coords[:8] * coords[:8]
    norm = -0.5 * (jnp.sum(squares, 0, keepdims=True) + ninth * ninth)
    norm_parts = split3(norm)
    half = jnp.full((1, width), -0.5, F32)
    side = jnp.concatenate(
        (
            jnp.zeros((8, width), F32), coords[:8], jnp.full((16, width), -0.5, F32),
            ninth, half, half, *norm_parts, jnp.zeros((128 - 38, width), F32),
        ), 0,
    )
    row_factor[...] = jnp.transpose(side)[:, :48].astype(BF16)

    def exponent(factor, dest):
        dest[...] = jnp.exp2(
            exponent_scale * jnp.dot(row_factor[...], factor[...], preferred_element_type=F32)
        ).astype(BF16)

    def spread(places):
        for place in places:
            if place != HOME:
                along(place).start()

    def relay(places):
        for place in places:
            if place != HOME:
                arrived(place, quad)
            over(place).start()
            aside(place).start()

    def relay_across(places):
        for place in places:
            arrived(place, across_quad)
            aside_across(place).start()

    def settle(places):
        for place in places:
            arrived(place, mate_quad)
            arrived(place, lax.rem(mate_quad + 2, QUAD))

    arrived(HOME, quad)
    spread(range(NEAR))
    relay((HOME,))

    backs[tiles] = jnp.zeros(backs.shape[1:], BF16)

    def member_at(position):
        place = position // QUAD
        d = jnp.int32(ORDER[0])
        for i in range(1, rows):
            d = jnp.where(place == i, ORDER[i], d)
        return at(y + d, lax.rem(position, QUAD))

    def find(position, count):
        k = member_at(position)
        hit = jnp.int32(0)
        for t in range(tiles):
            hit = jnp.where(listed_ref[0, 0, t] == k, 1, hit)
        inverse[position] = jnp.where(hit == 1, count, tiles)
        return count + hit

    lax.fori_loop(0, members, find, jnp.int32(0))

    def order(t, _):
        position = jnp.int32(0)
        for p in range(members):
            position = jnp.where(inverse[p] == t, p, position)
        sequence[t] = position
        return 0

    lax.fori_loop(0, tiles, order, 0)

    relay([place for place in range(NEAR) if place != HOME])

    fill_factor(own[:, :width], own[:, width:], factor_a)
    exponent(factor_a, tile_a)

    def towards_near(block, tile):
        return lax.dot_general(block, tile[...], (((1,), (1,)), ((), ())), preferred_element_type=F32)

    total[...] = noise_level * probe_values + towards_near(own[0:8, :width], tile_a)
    near[...] = jnp.zeros_like(near)

    relay_across(range(NEAR))
    settle(range(NEAR))

    def meet(step):
        for group in (g + (1 << step), g + group_count - (1 << step)):
            pl.semaphore_signal(
                met.at[step], inc=1, device_id={"group": lax.rem(group, group_count), "member": m}, device_id_type=MESH
            )

    meet(0)
    spread(range(NEAR, rows))

    def block_near(t):
        return near_panel[jnp.minimum(sequence[t], close - 1)]

    def block_any(t):
        position = sequence[t]
        a = near_panel[jnp.minimum(position, close - 1)]
        b = far_panel[jnp.maximum(position - close, 0)]
        return jnp.where(position < close, a, b)

    def prepare(block, factor):
        fill_factor(block[:, :width], block[:, width:], factor)

    half_width = width // 2

    def add_near(block, tile):
        near[...] += towards_near(block, tile)

    def keep_back(t, tile):
        back = jnp.dot(own[0:8, :width], tile[...], preferred_element_type=F32)
        backs[t] = jnp.concatenate((back[:, :half_width], back[:, half_width:]), 0).astype(BF16)

    def products(t, factor, tile):
        add_near(factor[0:8, :], tile)
        keep_back(t, tile)

    def back_copy(position, box, slot):
        return pltpu.make_async_remote_copy(
            src_ref=outbox.at[box], dst_ref=inbox.at[slot], send_sem=back_send, recv_sem=back_recv,
            device_id={"group": nxt, "member": member_at(position)}, device_id_type=MESH,
        )

    def give_back(position):
        outbox[position] = backs[inverse[position]]
        back_copy(position, position, position // QUAD * QUAD + quad).start()

    prepare(block_near(0), factor_a)
    exponent(factor_a, tile_a)
    prepare(block_near(1), factor_b)

    def pair(u, block):
        products(2 * u, factor_a, tile_a)
        exponent(factor_b, tile_b)
        prepare(block(2 * u + 2), factor_a)
        products(2 * u + 1, factor_b, tile_b)
        exponent(factor_a, tile_a)
        prepare(block(2 * u + 3), factor_b)

        @pl.when(2 * u < single)
        def _():
            give_back(2 * u)
            give_back(2 * u + 1)


    early = 3

    def early_pair(u, _):
        pair(u, block_near)
        for step, acts in enumerate(((), (relay,), (relay_across, settle))):

            @pl.when(u == step)
            def _(step=step, acts=acts):
                for act in acts:
                    act([place for place in range(NEAR, rows) if act != relay or place != HOME])
                pl.semaphore_wait(met.at[step], 2)
                if step < 2:
                    meet(step + 1)

        return 0

    def late_pair(u, _):
        pair(u, block_any)
        return 0

    lax.fori_loop(0, early, early_pair, 0)
    lax.fori_loop(early, tiles // 2 - 1, late_pair, 0)
    products(tiles - 2, factor_a, tile_a)
    exponent(factor_b, tile_b)
    add_near(factor_b[0:8, :], tile_b)

    weighted = probe_values * (total[...] + 2.0 * near[...])
    local = weighted[:, :128]
    for q in range(1, width // 128):
        local = local + weighted[:, q * 128 : (q + 1) * 128]
    line = lax.broadcasted_iota(jnp.int32, local.shape, 0)
    lane = lax.broadcasted_iota(jnp.int32, local.shape, 1)
    sums = jnp.where(line == lane, jnp.sum(local, 1, keepdims=True), 0.0)
    cur_own[...] = jnp.sum(sums, 0, keepdims=True)
    cur_in[0] = cur_own[...]

    def cur_copy(i):
        peer = lax.rem(m + i, members)
        return pltpu.make_async_remote_copy(
            src_ref=cur_own, dst_ref=cur_in.at[i], send_sem=cur_send, recv_sem=cur_recv,
            device_id={"group": g, "member": peer}, device_id_type=MESH,
        )

    def all_copy(i):
        return pltpu.make_async_remote_copy(
            src_ref=cur_group, dst_ref=cur_all.at[i], send_sem=all_send, recv_sem=all_recv,
            device_id={"group": lax.rem(g + i, group_count), "member": m}, device_id_type=MESH,
        )

    def each(first, last, step):
        def body(i, _):
            step(i)
            return 0

        lax.fori_loop(first, last, body, 0, unroll=True)

    def whole(ref, send_sem, recv_sem):
        return pltpu.make_async_remote_copy(
            src_ref=ref, dst_ref=ref, send_sem=send_sem, recv_sem=recv_sem,
            device_id={"group": g, "member": mate}, device_id_type=MESH,
        )

    each(1, members, lambda i: cur_copy(i).start())

    keep_back(tiles - 1, tile_b)

    core = lax.rem(quad, 2)
    shared = (members - single) // 2

    def hand_over(j):
        mate_out[j] = backs[inverse[single + 2 * j + 1 - core]]
        pltpu.make_async_remote_copy(
            src_ref=mate_out.at[j], dst_ref=mate_in.at[j], send_sem=mate_send, recv_sem=mate_recv,
            device_id={"group": g, "member": mate}, device_id_type=MESH,
        ).start()

    def give_sum(i):
        j = shared - 1 - i
        position = single + 2 * j + core
        sums = backs[inverse[position]].astype(F32) + mate_in[j].astype(F32)
        outbox[single + j] = sums.astype(BF16)
        back_copy(position, single + j, single + j // 2 * 2 + quad // 2).start()

    each(0, shared, hand_over)
    whole(mate_in, mate_send, mate_recv).wait_recv()
    each(0, shared, give_sum)


    rest = pl.ds(1, members - 1)
    whole(cur_in.at[rest], cur_send, cur_recv).wait_recv()
    cur_group[...] = jnp.sum(cur_in[...], 0)
    cur_all[0] = cur_group[...]
    each(1, group_count, lambda i: all_copy(i).start())

    whole(near_panel, gather_send.at[0], gather_recv.at[0]).wait_send()
    whole(far_panel, gather_send.at[1], gather_recv.at[0]).wait_send()
    whole(cur_in.at[rest], cur_send, cur_recv).wait_send()
    whole(mate_out, mate_send, mate_recv).wait_send()
    whole(outbox, back_send, back_recv).wait_send()
    others = cur_all.at[pl.ds(1, group_count - 1)]
    whole(others, all_send, all_recv).wait_send()

    whole(inbox, back_send, back_recv).wait_recv()
    share = inbox[0].astype(F32)
    for k in range(1, inbox.shape[0]):
        share = share + inbox[k].astype(F32)
    product_ref[...] = total[...] + near[...] + jnp.concatenate((share[:8], share[8:]), 1)

    whole(others, all_send, all_recv).wait_recv()
    curvature_ref[...] = jnp.sum(cur_all[...], 0) * (1.0 / (width * members * group_count))


def body(points, probes, col_blocks):
    width, dims, rhs = points.shape[1], points.shape[0], probes.shape[0]
    members, groups, tiles = lax.axis_size("member"), lax.axis_size("group"), col_blocks.shape[2]
    rows = members // QUAD
    boxes = (members + SINGLE * QUAD) // 2
    vmem = pl.BlockSpec(memory_space=pltpu.VMEM)
    dma = pltpu.SemaphoreType.DMA
    product, curvature = pl.pallas_call(
        functools.partial(kernel, dims, groups),
        out_shape=(jax.ShapeDtypeStruct((rhs, width), F32), jax.ShapeDtypeStruct((1, 128), F32)),
        in_specs=[vmem, vmem, pl.BlockSpec(memory_space=pltpu.SMEM)],
        out_specs=(vmem, vmem),
        scratch_shapes=[
            pltpu.VMEM((NEAR * QUAD, 16, width + 128), BF16),
            pltpu.VMEM((members - NEAR * QUAD, 16, width + 128), BF16),
            pltpu.VMEM((16, width + 128), BF16),
            pltpu.VMEM((rhs, width), F32),
            pltpu.VMEM((rhs, width), F32),
            pltpu.VMEM((tiles + 1, 16, width // 2), BF16),
            *[pltpu.VMEM((boxes, 16, width // 2), BF16)] * 2,
            *[pltpu.VMEM(((members - SINGLE * QUAD) // 2, 16, width // 2), BF16)] * 2,
            pltpu.VMEM((width, 48), BF16),
            pltpu.VMEM((48, width), BF16),
            pltpu.VMEM((48, width), BF16),
            *[pltpu.VMEM((width, width), BF16)] * 2,
            pltpu.SMEM((members,), jnp.int32),
            pltpu.SMEM((tiles,), jnp.int32),
            pltpu.VMEM((1, 128), F32),
            pltpu.VMEM((members, 1, 128), F32),
            pltpu.VMEM((1, 128), F32),
            pltpu.VMEM((groups, 1, 128), F32),
            pltpu.SemaphoreType.REGULAR((3,)), dma((2,)), dma((members,)),
            *[dma] * 8,
        ],
        compiler_params=pltpu.CompilerParams(
            collective_id=0, has_side_effects=True, vmem_limit_bytes=48 * 2**20
        ),
    )(points, probes, col_blocks)
    return product, curvature[0, :rhs]


def solution(mesh):
    return jax.shard_map(
        body,
        mesh=mesh,
        in_specs=(
            P(None, ("group", "member")),
            P(None, ("group", "member")),
            P("group", "member", None),
        ),
        out_specs=(P(None, ("group", "member")), P()),
        check_vma=False,
    )
```
